32 devices in a mesh: section: 4 (over y, x), row: 4 (over z), col: 2 (over core).
Axes of the slice: x: 2, y: 2, z: 4, core: 2. Of those that a mesh axis runs over, the one named last changes fastest.
Arguments:
- statistic: float32 [8192, 2048], P(('section', 'row'), 'col'), parts along dimension 0, as said below
- gradient: bfloat16 [8192, 28672], P('section', ('row', 'col')), parts along dimension 0, may hold values from -6 to 6
Outputs:
- next_m: float32 [8192, 2048], P(('section', 'row'), 'col'), parts along dimension 0
- preconditioned: bfloat16 [8192, 28672], P('section', ('row', 'col')), parts along dimension 0
- next_diag: float32 [8192], P(('section', 'row')), parts along dimension 0
The draws below stay inside these ranges and needn't reach their ends.
There are 4 independent parts, one for each index of `section`. The reference program is written for one: setup_inputs(seed, part) draws one part's arguments, and reference() takes and returns one part's arrays. A program takes and returns all parts, laid end to end along the dimension named above; each array names one. Nothing has to cross between parts.
Inputs may be any that keep to these rules, and one draw needn't show every extreme that they name: `statistic`: symmetric and positive definite.
All inputs are finite; a program needn't handle non-finite values.
Results may differ from the reference program's by a relative error of at most 0.0052.
Values may be sent and summed in bfloat16 or wider, within the bound.
A program may use at most 128 MiB of HBM per device.

```python
import math
import jax
import jax.numpy as jnp
from jax import lax

BLOCK = 2048
FF = 28672


def draw_statistic(key, part):
    first, second = jax.random.split(jax.random.fold_in(key, 11), 2)
    places = jnp.arange(BLOCK, dtype=jnp.float32)
    ramp = 1.0 + 2.0 * places / BLOCK
    noise = jax.random.normal(first, (BLOCK, BLOCK), jnp.float32)
    scales = ramp * jnp.exp(jax.random.uniform(second, (BLOCK,), jnp.float32, 0.0, math.log(6.0)))
    symmetric = (noise + noise.T) * (0.70710678 / math.sqrt(BLOCK))
    inner = symmetric + 2.5 * jnp.eye(BLOCK, dtype=jnp.float32)
    roots = jnp.sqrt(scales)
    return roots[:, None] * inner * roots[None, :]


def level_of(rng, dims, pieces, least, top_value):
    level = 1.0
    for dim, parts in pieces:
        steps = jax.random.uniform(jax.random.fold_in(jax.random.fold_in(rng, 6), dim), (parts,), jnp.float32, least / len(pieces), top_value / len(pieces))
        level = level * jnp.repeat(jnp.exp(steps), dims[dim] // parts).reshape((-1,) + (1,) * (len(dims) - 1 - dim))
    return level


def normal_values(key, dims, spread, most, pieces=(), kind=jnp.bfloat16):
    gain = level_of(key, dims, pieces, -0.22, 0.18) if pieces else 1.0
    entries = jax.random.normal(key, dims, jnp.float32) * spread * gain
    return jnp.minimum(jnp.maximum(entries, -most), most).astype(kind)


def setup_inputs(seed: int = 0, part: int = 0) -> dict:
    arg_keys = jax.random.split(jax.random.key(seed), 3)
    part_splits = jax.random.split(jax.random.fold_in(arg_keys[2], part), 3)
    statistic = draw_statistic(jax.random.fold_in(jax.random.fold_in(arg_keys[2], part), 71), part)
    gradient = normal_values(part_splits[1], (BLOCK, FF), 1.0, 6.0, ((1, 8),))
    return dict(statistic=statistic, gradient=gradient)


def reference(statistic, gradient):
    highest = lax.Precision.HIGHEST
    total = jnp.sum(statistic * statistic)
    scale4 = jnp.sqrt(BLOCK * (total / (BLOCK * BLOCK) + 1e-06))
    m_start = statistic / scale4
    ident = jnp.eye(BLOCK, dtype=jnp.float32)
    t_mat = (5.0 * ident - m_start) / 4.0
    square = jnp.dot(t_mat, t_mat, precision=highest, preferred_element_type=jnp.float32)
    third = jnp.dot(square, m_start, precision=highest, preferred_element_type=jnp.float32)
    full = jnp.dot(square, third, precision=highest, preferred_element_type=jnp.float32)
    next_m = full * (1.0 - ident)
    next_diag = jnp.diagonal(full)
    x_next = (t_mat / jnp.sqrt(jnp.sqrt(scale4))).astype(jnp.bfloat16)
    preconditioned = jnp.dot(x_next, gradient, preferred_element_type=jnp.float32).astype(jnp.bfloat16)
    return (next_m, preconditioned, next_diag)
```

```python
import functools

import jax
import jax.numpy as jnp
from jax import lax
from jax.experimental import pallas as pl
from jax.experimental.pallas import tpu as pltpu
from jax.sharding import PartitionSpec as P

F32, BF16 = jnp.float32, jnp.bfloat16
MIB = 1024 * 1024


def split(extent, most):
    step = most
    while extent % step:
        step -= 128
    return step


def coefficients(total, n):
    scale4 = jnp.sqrt(n * (total / (n * n) + 1e-06))
    return scale4, jnp.sqrt(jnp.sqrt(scale4))


def exchange_kernel(
    R, C, s_ref, g_ref, y_ref, sf_out, info_out,
    sf, gv, yv, mine, notes,
    g_sem, y_sem, o_sem, send_sem, fwd_sem, recv_sem, note_send, note_recv,
):
    z, c = lax.axis_index("row"), lax.axis_index("col")
    bs, width = s_ref.shape
    n = sf.shape[0]
    nf = gv.shape[1]
    H = R // C
    sib = 1 - c

    def block(ref, a, b):
        return ref.at[
            pl.ds(pl.multiple_of(a * bs, bs), bs), pl.ds(pl.multiple_of(b * bs, bs), bs)
        ]

    def chosen(s, o, t):
        ds, do = jnp.abs(s - t), jnp.abs(o - t)
        low = jnp.where(t < R // 2, 1, 0)
        tie = jnp.where(low == 1, jnp.where(s < o, 1, 0), jnp.where(s > o, 1, 0))
        pick = jnp.where(ds < do, 1, jnp.where(ds == do, tie, 0))
        return jnp.where(s == o, 1, pick)

    def sends(p, act):
        def body(idx, carry):
            h, side = idx // 2, idx % 2
            t = z + p * (2 * side - 1)
            b = c * H + h
            ok = (t >= 0) & (t < R) & (t != b)

            @pl.when(ok & (chosen(z, b, t) == 1))
            def _():
                act(
                    pltpu.make_async_remote_copy(
                        src_ref=block(sf, z, b), dst_ref=block(sf, z, b),
                        send_sem=send_sem.at[p, h, side], recv_sem=recv_sem.at[z, b],
                        device_id={"row": t, "col": c},
                        device_id_type=pl.DeviceIdType.MESH,
                    )
                )
            return carry
        lax.fori_loop(0, 2 * H, body, 0)

    def to_sibling(a, b):
        return pltpu.make_async_remote_copy(
            src_ref=block(sf, a, b), dst_ref=block(sf, a, b),
            send_sem=fwd_sem.at[a, b], recv_sem=recv_sem.at[a, b],
            device_id={"col": sib}, device_id_type=pl.DeviceIdType.MESH,
        )

    def mirror(s, o):
        @pl.when(s != o)
        def _():
            block(sf, o, s)[...] = block(sf, s, o)[...].T

    def arrivals(p):
        for direct in (True, False):
            def body(idx, carry):
                side, h = idx // H, idx % H
                s = z + p * (2 * side - 1)
                o = (c if direct else sib) * H + h
                ok = (s >= 0) & (s < R) & (o != z)

                @pl.when(ok & (chosen(s, o, z) == 1))
                def _():
                    to_sibling(s, o).wait_recv()
                    if direct:
                        to_sibling(s, o).start()
                    mirror(s, o)
                return carry
            lax.fori_loop(0, 2 * H, body, 0)

    def forwards_done(p):
        def body(idx, carry):
            side, h = idx // H, idx % H
            s = z + p * (2 * side - 1)
            o = c * H + h
            ok = (s >= 0) & (s < R) & (o != z)

            @pl.when(ok & (chosen(s, o, z) == 1))
            def _():
                to_sibling(s, o).wait_send()
            return carry
        lax.fori_loop(0, 2 * H, body, 0)

    def g_copy(k):
        rows = pl.ds(k * bs, bs)
        return pltpu.make_async_copy(g_ref.at[rows], gv.at[rows], g_sem.at[k])

    for k in range(R):
        g_copy(k).start()

    barrier = pltpu.get_barrier_semaphore()
    for dz in range(R):
        for dc in range(C):
            if dz or dc:
                pl.semaphore_signal(
                    barrier, inc=1,
                    device_id={"row": lax.rem(z + dz, R), "col": lax.rem(c + dc, C)},
                    device_id_type=pl.DeviceIdType.MESH,
                )

    rows_z = pl.ds(pl.multiple_of(z * bs, bs), bs)
    for h in range(H):
        block(sf, z, c * H + h)[...] = s_ref[:, h * bs:(h + 1) * bs].astype(BF16)
    pl.semaphore_wait(barrier, R * C - 1)
    for h in range(H):
        to_sibling(z, c * H + h).start()
    sends(1, lambda d: d.start())

    step = min(bs, 64)

    def scan(r, carry):
        acc, low = carry
        at = pl.multiple_of(r * step, step)
        s = s_ref[pl.ds(at, step), :]
        acc = acc + jnp.sum((s * s).reshape(step // 8, 8, width), axis=0)
        ri = lax.broadcasted_iota(jnp.int32, (step, width), 0) + (z * bs + at)
        ci = lax.broadcasted_iota(jnp.int32, (step, width), 1) + c * width
        left = jnp.where(ri == ci, s - s.astype(BF16).astype(F32), 0.0)
        low = low + jnp.sum(left.reshape(step // 8, 8, width), axis=0)
        return acc, low

    zero = jnp.zeros((8, width), F32)
    acc, low = lax.fori_loop(0, bs // step, scan, (zero, zero))
    mine[:, pl.ds(0, width)] = jnp.sum(low, axis=0, keepdims=True)
    own_total = jnp.sum(jnp.sum(acc, axis=0, keepdims=True), axis=1, keepdims=True)
    mine[:, pl.ds(width, 128)] = jnp.broadcast_to(own_total, (1, 128))

    def note_copy(dz, dc):
        return pltpu.make_async_remote_copy(
            src_ref=mine, dst_ref=notes.at[dz, dc],
            send_sem=note_send.at[dz, dc], recv_sem=note_recv.at[dz, dc],
            device_id={"row": lax.rem(z + dz, R), "col": lax.rem(c + dc, C)},
            device_id_type=pl.DeviceIdType.MESH,
        )

    others = [(dz, dc) for dz in range(R) for dc in range(C) if dz or dc]
    for dz, dc in others:
        note_copy(dz, dc).start()
    notes[0, 0] = mine[...]

    for h in range(H):
        to_sibling(z, sib * H + h).wait_recv()

    def own_mirror(o, carry):
        mirror(z, o)
        return carry
    lax.fori_loop(0, R, own_mirror, 0)

    for k in range(R):
        g_copy(k).wait()
    for dz, dc in others:
        note_copy(dz, dc).wait_recv()
    near = functools.reduce(lambda a, b: a + b, [notes[d, 0] for d in range(R)])
    far = functools.reduce(lambda a, b: a + b, [notes[d, 1] for d in range(R)])
    total = near[:, width:] + far[:, width:]
    info_out[:, pl.ds(pl.multiple_of(c * width, 128), width)] = near[:, :width]
    info_out[:, pl.ds(pl.multiple_of(sib * width, 128), width)] = far[:, :width]
    info_out[:, pl.ds(n, 128)] = total
    scale4, root = coefficients(total[:, :1], n)
    keep, take = 1.25 / root, (0.25 / scale4) / root
    chunk = split(nf, 512)

    def y_copy(i):
        rows = pl.ds(pl.multiple_of(i * bs, bs), bs)
        return pltpu.make_async_copy(yv.at[rows], y_ref.at[rows], y_sem.at[i])

    def compute(i):
        rows = pl.ds(pl.multiple_of(i * bs, bs), bs)

        def body(j, carry):
            cols = pl.ds(pl.multiple_of(j * chunk, chunk), chunk)
            prod = jnp.dot(sf[rows, :], gv[:, cols], preferred_element_type=F32)
            yv[rows, cols] = (keep * gv[rows, cols].astype(F32) - take * prod).astype(BF16)
            return carry
        lax.fori_loop(0, nf // chunk, body, 0)
        y_copy(i).start()

    compute(z)
    for p in range(1, R):
        arrivals(p)
        sends(p, lambda d: d.wait_send())
        if p + 1 < R:
            sends(p + 1, lambda d: d.start())
        else:
            whole = pltpu.make_async_copy(sf, sf_out, o_sem)
            whole.start()

        def both(side, carry):
            i = z + p * (2 * side - 1)

            @pl.when((i >= 0) & (i < R))
            def _():
                compute(i)
            return carry
        lax.fori_loop(0, 2, both, 0)

    for h in range(H):
        to_sibling(z, c * H + h).wait_send()
    for p in range(1, R):
        forwards_done(p)
    for dz, dc in others:
        note_copy(dz, dc).wait_send()
    for i in range(R):
        y_copy(i).wait()
    whole.wait()


def newton_kernel(
    R, C, y_ref, sf, s_ref, info_ref, pre_ref, next_ref, diag_ref,
    held, narrow, y_sem,
):
    z, c = lax.axis_index("row"), lax.axis_index("col")
    bs, width = s_ref.shape
    n = sf.shape[0]

    def y_copy(i):
        rows = pl.ds(i * bs, bs)
        return pltpu.make_async_copy(y_ref.at[rows], pre_ref.at[rows], y_sem.at[i])

    for i in range(R):
        y_copy(i).start()

    scale4, _ = coefficients(info_ref[:, pl.ds(n, 1)], n)
    inv = 1.0 / scale4
    chunk = split(width, 512)
    rows_z = pl.ds(pl.multiple_of(z * bs, bs), bs)

    def ident(at, size):
        ri = lax.broadcasted_iota(jnp.int32, (bs, size), 0) + z * bs
        ci = lax.broadcasted_iota(jnp.int32, (bs, size), 1) + at
        return ri == ci

    def first(j, carry):
        at = pl.multiple_of(j * chunk, chunk)
        cols = pl.ds(at, chunk)
        m = sf[rows_z, cols].astype(F32)
        m = (m + jnp.where(ident(at, chunk), info_ref[:, cols], 0.0)) * inv
        held[0, :, cols] = m
        narrow[0, :, cols] = m.astype(BF16)
        return carry
    lax.fori_loop(0, n // chunk, first, 0)

    def product(now, at):
        cols = pl.ds(at, chunk)
        prod = jnp.dot(narrow[now], sf[:, cols], preferred_element_type=F32)
        r = held[now, :, cols]
        return 1.25 * r - (0.25 * inv) * (prod + r * info_ref[:, cols])

    def turn(step, carry):
        now, later = step % 2, (step + 1) % 2

        def body(j, inner):
            at = pl.multiple_of(j * chunk, chunk)
            r = product(now, at)
            held[later, :, pl.ds(at, chunk)] = r
            narrow[later, :, pl.ds(at, chunk)] = r.astype(BF16)
            return inner
        lax.fori_loop(0, n // chunk, body, 0)
        return carry
    lax.fori_loop(0, 3, turn, 0)

    def last(j, carry):
        at = pl.multiple_of(c * width + j * chunk, chunk)
        r = product(1, at)
        next_ref[:, pl.ds(pl.multiple_of(j * chunk, chunk), chunk)] = jnp.where(
            ident(at, chunk), 0.0, r
        )
        return carry
    lax.fori_loop(0, width // chunk, last, 0)

    def diagonal(j, carry):
        at = pl.multiple_of(j * chunk, chunk)
        cols = pl.ds(at, chunk)
        r = held[1, :, cols]
        on = ident(at, chunk)
        s = sf[rows_z, cols].astype(F32) + jnp.where(on, info_ref[:, cols], 0.0)
        term = jnp.where(on, 1.25 * r, 0.0) - (0.25 * inv) * (r * s)
        return carry + jnp.sum(term, axis=1, keepdims=True)
    diag_ref[...] = lax.fori_loop(0, n // chunk, diagonal, jnp.zeros((bs, 1), F32))

    for i in range(R):
        y_copy(i).wait()


def local_kernels(R, C, statistic, gradient):
    bs, width = statistic.shape
    n, nf = gradient.shape
    vmem, hbm = pl.BlockSpec(memory_space=pltpu.VMEM), pl.BlockSpec(memory_space=pl.ANY)
    dma = pltpu.SemaphoreType.DMA
    H = R // C
    y, sf, info = pl.pallas_call(
        functools.partial(exchange_kernel, R, C),
        out_shape=(
            jax.ShapeDtypeStruct((n, nf), BF16),
            jax.ShapeDtypeStruct((n, n), BF16),
            jax.ShapeDtypeStruct((1, n + 128), F32),
        ),
        in_specs=[vmem, hbm],
        out_specs=(hbm, hbm, vmem),
        scratch_shapes=[
            pltpu.VMEM((n, n), BF16),
            pltpu.VMEM((n, nf), BF16),
            pltpu.VMEM((n, nf), BF16),
            pltpu.VMEM((1, width + 128), F32),
            pltpu.VMEM((R, C, 1, width + 128), F32),
            dma((R,)), dma((R,)), dma,
            dma((R, H, 2)), dma((R, R)), dma((R, R)),
            dma((R, C)), dma((R, C)),
        ],
        compiler_params=pltpu.CompilerParams(
            collective_id=0, has_side_effects=True, vmem_limit_bytes=56 * MIB
        ),
        cost_estimate=pl.CostEstimate(
            flops=2 * n * n * nf, bytes_accessed=4 * n * nf, transcendentals=0
        ),
        name="exchange",
    )(statistic, gradient)
    pre, next_m, diag = pl.pallas_call(
        functools.partial(newton_kernel, R, C),
        out_shape=(
            jax.ShapeDtypeStruct((n, nf), BF16),
            jax.ShapeDtypeStruct((bs, width), F32),
            jax.ShapeDtypeStruct((bs, 1), F32),
        ),
        in_specs=[hbm, vmem, vmem, vmem],
        out_specs=(hbm, vmem, vmem),
        scratch_shapes=[
            pltpu.VMEM((2, bs, n), F32),
            pltpu.VMEM((2, bs, n), BF16),
            dma((R,)),
        ],
        compiler_params=pltpu.CompilerParams(vmem_limit_bytes=48 * MIB),
        cost_estimate=pl.CostEstimate(
            flops=8 * bs * n * n, bytes_accessed=4 * n * nf, transcendentals=0
        ),
        name="newton",
    )(y, sf, statistic, info)
    return next_m, pre, diag.reshape(bs)


def local_plain(statistic, gradient):
    n = gradient.shape[0]
    rows_here, cols_here = statistic.shape
    total = lax.psum(jnp.sum(statistic * statistic), ("row", "col"))
    scale4, root = coefficients(total, n)
    row_ids = lax.axis_index("row") * rows_here + jnp.arange(rows_here, dtype=jnp.int32)
    col_start = lax.axis_index("col") * cols_here
    col_ids = col_start + jnp.arange(cols_here, dtype=jnp.int32)
    own = row_ids[:, None] == col_ids[None, :]
    left = jnp.where(own, statistic - statistic.astype(BF16).astype(F32), 0.0)
    low_here = lax.dynamic_update_slice(
        jnp.zeros((n,), F32), jnp.sum(left, axis=0), (col_start,)
    )
    low = lax.psum(low_here, ("row", "col"))
    wide = lax.all_gather(statistic.astype(BF16), "col", axis=1, tiled=True)
    whole = lax.all_gather(wide, "row", axis=0, tiled=True)
    prod = jnp.dot(whole, gradient, preferred_element_type=F32)
    pre = ((1.25 * gradient.astype(F32) - prod * (0.25 / scale4)) / root).astype(BF16)
    every = jnp.arange(n, dtype=jnp.int32)
    ident = row_ids[:, None] == every[None, :]
    r = (wide.astype(F32) + jnp.where(ident, low[None, :], 0.0)) / scale4
    for _ in range(4):
        prod = jnp.dot(r.astype(BF16), whole, preferred_element_type=F32)
        r = 1.25 * r - 0.25 * (prod + r * low[None, :]) / scale4
    next_diag = jnp.sum(jnp.where(ident, r, 0.0), axis=1)
    next_m = jnp.where(own, 0.0, lax.dynamic_slice_in_dim(r, col_start, cols_here, 1))
    return next_m, pre, next_diag


def solution(mesh):
    R, C = mesh.shape["row"], mesh.shape["col"]
    local = functools.partial(local_kernels, R, C) if C == 2 and R % C == 0 else local_plain
    return jax.shard_map(
        local,
        mesh=mesh,
        in_specs=(P(("section", "row"), "col"), P("section", ("row", "col"))),
        out_specs=(
            P(("section", "row"), "col"),
            P("section", ("row", "col")),
            P(("section", "row")),
        ),
        check_vma=False,
    )
```

```python
import functools

import jax
import jax.numpy as jnp
from jax import lax
from jax.experimental import pallas as pl
from jax.experimental.pallas import tpu as pltpu
from jax.sharding import PartitionSpec as P

F32, BF16 = jnp.float32, jnp.bfloat16
MIB = 1024 * 1024


def split(extent, most):
    step = most
    while extent % step:
        step -= 128
    return step


def coefficients(total, n):
    scale4 = jnp.sqrt(n * (total / (n * n) + 1e-06))
    return scale4, jnp.sqrt(jnp.sqrt(scale4))


def exchange_kernel(
    R, C, s_ref, g_ref, y_ref, sf_out, info_out,
    sf, gv, yv, mine, notes,
    g_sem, y_sem, o_sem, send_sem, fwd_sem, recv_sem, note_send, note_recv,
):
    z, c = lax.axis_index("row"), lax.axis_index("col")
    bs, width = s_ref.shape
    n = sf.shape[0]
    nf = gv.shape[1]
    H = R // C
    sib = 1 - c

    def block(ref, a, b):
        return ref.at[
            pl.ds(pl.multiple_of(a * bs, bs), bs), pl.ds(pl.multiple_of(b * bs, bs), bs)
        ]

    def chosen(s, o, t):
        ds, do = jnp.abs(s - t), jnp.abs(o - t)
        low = jnp.where(t < R // 2, 1, 0)
        tie = jnp.where(low == 1, jnp.where(s < o, 1, 0), jnp.where(s > o, 1, 0))
        pick = jnp.where(ds < do, 1, jnp.where(ds == do, tie, 0))
        return jnp.where(s == o, 1, pick)

    def sends(p, act):
        def body(idx, carry):
            h, side = idx // 2, idx % 2
            t = z + p * (2 * side - 1)
            b = c * H + h
            ok = (t >= 0) & (t < R) & (t != b)

            @pl.when(ok & (chosen(z, b, t) == 1))
            def _():
                act(
                    pltpu.make_async_remote_copy(
                        src_ref=block(sf, z, b), dst_ref=block(sf, z, b),
                        send_sem=send_sem.at[p, h, side], recv_sem=recv_sem.at[z, b],
                        device_id={"row": t, "col": c},
                        device_id_type=pl.DeviceIdType.MESH,
                    )
                )
            return carry
        lax.fori_loop(0, 2 * H, body, 0)

    def to_sibling(a, b):
        return pltpu.make_async_remote_copy(
            src_ref=block(sf, a, b), dst_ref=block(sf, a, b),
            send_sem=fwd_sem.at[a, b], recv_sem=recv_sem.at[a, b],
            device_id={"col": sib}, device_id_type=pl.DeviceIdType.MESH,
        )

    def mirror(s, o):
        @pl.when(s != o)
        def _():
            block(sf, o, s)[...] = block(sf, s, o)[...].T

    def arrivals(p):
        for direct in (True, False):
            def body(idx, carry):
                side, h = idx // H, idx % H
                s = z + p * (2 * side - 1)
                o = (c if direct else sib) * H + h
                ok = (s >= 0) & (s < R) & (o != z)

                @pl.when(ok & (chosen(s, o, z) == 1))
                def _():
                    to_sibling(s, o).wait_recv()
                    if direct:
                        to_sibling(s, o).start()
                    mirror(s, o)
                return carry
            lax.fori_loop(0, 2 * H, body, 0)

    def forwards_done(p):
        def body(idx, carry):
            side, h = idx // H, idx % H
            s = z + p * (2 * side - 1)
            o = c * H + h
            ok = (s >= 0) & (s < R) & (o != z)

            @pl.when(ok & (chosen(s, o, z) == 1))
            def _():
                to_sibling(s, o).wait_send()
            return carry
        lax.fori_loop(0, 2 * H, body, 0)

    def g_copy(k):
        rows = pl.ds(k * bs, bs)
        return pltpu.make_async_copy(g_ref.at[rows], gv.at[rows], g_sem.at[k])

    for k in range(R):
        g_copy(k).start()

    barrier = pltpu.get_barrier_semaphore()
    for dz in range(R):
        for dc in range(C):
            if dz or dc:
                pl.semaphore_signal(
                    barrier, inc=1,
                    device_id={"row": lax.rem(z + dz, R), "col": lax.rem(c + dc, C)},
                    device_id_type=pl.DeviceIdType.MESH,
                )

    rows_z = pl.ds(pl.multiple_of(z * bs, bs), bs)
    for h in range(H):
        block(sf, z, c * H + h)[...] = s_ref[:, h * bs:(h + 1) * bs].astype(BF16)
    pl.semaphore_wait(barrier, R * C - 1)
    for h in range(H):
        to_sibling(z, c * H + h).start()
    sends(1, lambda d: d.start())

    step = min(bs, 64)

    def scan(r, carry):
        acc, low = carry
        at = pl.multiple_of(r * step, step)
        s = s_ref[pl.ds(at, step), :]
        acc = acc + jnp.sum((s * s).reshape(step // 8, 8, width), axis=0)
        ri = lax.broadcasted_iota(jnp.int32, (step, width), 0) + (z * bs + at)
        ci = lax.broadcasted_iota(jnp.int32, (step, width), 1) + c * width
        left = jnp.where(ri == ci, s - s.astype(BF16).astype(F32), 0.0)
        low = low + jnp.sum(left.reshape(step // 8, 8, width), axis=0)
        return acc, low

    zero = jnp.zeros((8, width), F32)
    acc, low = lax.fori_loop(0, bs // step, scan, (zero, zero))
    mine[:, pl.ds(0, width)] = jnp.sum(low, axis=0, keepdims=True)
    own_total = jnp.sum(jnp.sum(acc, axis=0, keepdims=True), axis=1, keepdims=True)
    mine[:, pl.ds(width, 128)] = jnp.broadcast_to(own_total, (1, 128))

    def note_copy(dz, dc):
        return pltpu.make_async_remote_copy(
            src_ref=mine, dst_ref=notes.at[dz, dc],
            send_sem=note_send.at[dz, dc], recv_sem=note_recv.at[dz, dc],
            device_id={"row": lax.rem(z + dz, R), "col": lax.rem(c + dc, C)},
            device_id_type=pl.DeviceIdType.MESH,
        )

    others = [(dz, dc) for dz in range(R) for dc in range(C) if dz or dc]
    for dz, dc in others:
        note_copy(dz, dc).start()
    notes[0, 0] = mine[...]

    for h in range(H):
        to_sibling(z, sib * H + h).wait_recv()

    def own_mirror(o, carry):
        mirror(z, o)
        return carry
    lax.fori_loop(0, R, own_mirror, 0)

    for k in range(R):
        g_copy(k).wait()
    for dz, dc in others:
        note_copy(dz, dc).wait_recv()
    near = functools.reduce(lambda a, b: a + b, [notes[d, 0] for d in range(R)])
    far = functools.reduce(lambda a, b: a + b, [notes[d, 1] for d in range(R)])
    total = near[:, width:] + far[:, width:]
    info_out[:, pl.ds(pl.multiple_of(c * width, 128), width)] = near[:, :width]
    info_out[:, pl.ds(pl.multiple_of(sib * width, 128), width)] = far[:, :width]
    info_out[:, pl.ds(n, 128)] = total
    scale4, root = coefficients(total[:, :1], n)
    keep, take = 1.25 / root, (0.25 / scale4) / root
    chunk = split(nf, 512)

    def y_copy(i):
        rows = pl.ds(pl.multiple_of(i * bs, bs), bs)
        return pltpu.make_async_copy(yv.at[rows], y_ref.at[rows], y_sem.at[i])

    def compute(i):
        rows = pl.ds(pl.multiple_of(i * bs, bs), bs)

        def body(j, carry):
            cols = pl.ds(pl.multiple_of(j * chunk, chunk), chunk)
            prod = jnp.dot(sf[rows, :], gv[:, cols], preferred_element_type=F32)
            yv[rows, cols] = (keep * gv[rows, cols].astype(F32) - take * prod).astype(BF16)
            return carry
        lax.fori_loop(0, nf // chunk, body, 0)
        y_copy(i).start()

    compute(z)
    for p in range(1, R):
        arrivals(p)
        sends(p, lambda d: d.wait_send())
        if p + 1 < R:
            sends(p + 1, lambda d: d.start())
        else:
            whole = pltpu.make_async_copy(sf, sf_out, o_sem)
            whole.start()

        def both(side, carry):
            i = z + p * (2 * side - 1)

            @pl.when((i >= 0) & (i < R))
            def _():
                compute(i)
            return carry
        lax.fori_loop(0, 2, both, 0)

    for h in range(H):
        to_sibling(z, c * H + h).wait_send()
    for p in range(1, R):
        forwards_done(p)
    for dz, dc in others:
        note_copy(dz, dc).wait_send()
    for i in range(R):
        y_copy(i).wait()
    whole.wait()


def newton_kernel(
    R, C, y_ref, sf, s_ref, info_ref, pre_ref, next_ref, diag_ref,
    held, narrow, yv, in_sem, out_sem,
):
    z, c = lax.axis_index("row"), lax.axis_index("col")
    bs, width = s_ref.shape
    n = sf.shape[0]

    def y_in(i):
        rows = pl.ds(i * bs, bs)
        return pltpu.make_async_copy(y_ref.at[rows], yv.at[rows], in_sem.at[i])

    def y_out(i):
        rows = pl.ds(i * bs, bs)
        return pltpu.make_async_copy(yv.at[rows], pre_ref.at[rows], out_sem.at[i])

    for i in range(R):
        y_in(i).start()

    scale4, _ = coefficients(info_ref[:, pl.ds(n, 1)], n)
    inv = 1.0 / scale4
    chunk = split(width, 512)
    rows_z = pl.ds(pl.multiple_of(z * bs, bs), bs)

    def ident(at, size):
        ri = lax.broadcasted_iota(jnp.int32, (bs, size), 0) + z * bs
        ci = lax.broadcasted_iota(jnp.int32, (bs, size), 1) + at
        return ri == ci

    def first(j, carry):
        at = pl.multiple_of(j * chunk, chunk)
        cols = pl.ds(at, chunk)
        m = sf[rows_z, cols].astype(F32)
        m = (m + jnp.where(ident(at, chunk), info_ref[:, cols], 0.0)) * inv
        held[0, :, cols] = m
        narrow[0, :, cols] = m.astype(BF16)
        return carry
    lax.fori_loop(0, n // chunk, first, 0)

    def product(now, at):
        cols = pl.ds(at, chunk)
        prod = jnp.dot(narrow[now], sf[:, cols], preferred_element_type=F32)
        r = held[now, :, cols]
        return 1.25 * r - (0.25 * inv) * (prod + r * info_ref[:, cols])

    def turn(step, carry):
        now, later = step % 2, (step + 1) % 2

        def body(j, inner):
            at = pl.multiple_of(j * chunk, chunk)
            r = product(now, at)
            held[later, :, pl.ds(at, chunk)] = r
            narrow[later, :, pl.ds(at, chunk)] = r.astype(BF16)
            return inner
        lax.fori_loop(0, n // chunk, body, 0)
        return carry
    turn(0, 0)
    for i in range(R):
        y_in(i).wait()
        y_out(i).start()
    lax.fori_loop(1, 3, turn, 0)

    def last(j, carry):
        at = pl.multiple_of(c * width + j * chunk, chunk)
        r = product(1, at)
        next_ref[:, pl.ds(pl.multiple_of(j * chunk, chunk), chunk)] = jnp.where(
            ident(at, chunk), 0.0, r
        )
        return carry
    lax.fori_loop(0, width // chunk, last, 0)

    def diagonal(j, carry):
        at = pl.multiple_of(j * chunk, chunk)
        cols = pl.ds(at, chunk)
        r = held[1, :, cols]
        on = ident(at, chunk)
        s = sf[rows_z, cols].astype(F32) + jnp.where(on, info_ref[:, cols], 0.0)
        term = jnp.where(on, 1.25 * r, 0.0) - (0.25 * inv) * (r * s)
        return carry + jnp.sum(term, axis=1, keepdims=True)
    diag_ref[...] = lax.fori_loop(0, n // chunk, diagonal, jnp.zeros((bs, 1), F32))

    for i in range(R):
        y_out(i).wait()


def local_kernels(R, C, statistic, gradient):
    bs, width = statistic.shape
    n, nf = gradient.shape
    vmem, hbm = pl.BlockSpec(memory_space=pltpu.VMEM), pl.BlockSpec(memory_space=pl.ANY)
    dma = pltpu.SemaphoreType.DMA
    H = R // C
    y, sf, info = pl.pallas_call(
        functools.partial(exchange_kernel, R, C),
        out_shape=(
            jax.ShapeDtypeStruct((n, nf), BF16),
            jax.ShapeDtypeStruct((n, n), BF16),
            jax.ShapeDtypeStruct((1, n + 128), F32),
        ),
        in_specs=[vmem, hbm],
        out_specs=(hbm, hbm, vmem),
        scratch_shapes=[
            pltpu.VMEM((n, n), BF16),
            pltpu.VMEM((n, nf), BF16),
            pltpu.VMEM((n, nf), BF16),
            pltpu.VMEM((1, width + 128), F32),
            pltpu.VMEM((R, C, 1, width + 128), F32),
            dma((R,)), dma((R,)), dma,
            dma((R, H, 2)), dma((R, R)), dma((R, R)),
            dma((R, C)), dma((R, C)),
        ],
        compiler_params=pltpu.CompilerParams(
            collective_id=0, has_side_effects=True, vmem_limit_bytes=56 * MIB
        ),
        cost_estimate=pl.CostEstimate(
            flops=2 * n * n * nf, bytes_accessed=4 * n * nf, transcendentals=0
        ),
        name="exchange",
    )(statistic, gradient)
    pre, next_m, diag = pl.pallas_call(
        functools.partial(newton_kernel, R, C),
        out_shape=(
            jax.ShapeDtypeStruct((n, nf), BF16),
            jax.ShapeDtypeStruct((bs, width), F32),
            jax.ShapeDtypeStruct((bs, 1), F32),
        ),
        in_specs=[hbm, vmem, vmem, vmem],
        out_specs=(hbm, vmem, vmem),
        scratch_shapes=[
            pltpu.VMEM((2, bs, n), F32),
            pltpu.VMEM((2, bs, n), BF16),
            pltpu.VMEM((n, nf), BF16),
            dma((R,)), dma((R,)),
        ],
        compiler_params=pltpu.CompilerParams(vmem_limit_bytes=56 * MIB),
        cost_estimate=pl.CostEstimate(
            flops=8 * bs * n * n, bytes_accessed=4 * n * nf, transcendentals=0
        ),
        name="newton",
    )(y, sf, statistic, info)
    return next_m, pre, diag.reshape(bs)


def local_plain(statistic, gradient):
    n = gradient.shape[0]
    rows_here, cols_here = statistic.shape
    total = lax.psum(jnp.sum(statistic * statistic), ("row", "col"))
    scale4, root = coefficients(total, n)
    row_ids = lax.axis_index("row") * rows_here + jnp.arange(rows_here, dtype=jnp.int32)
    col_start = lax.axis_index("col") * cols_here
    col_ids = col_start + jnp.arange(cols_here, dtype=jnp.int32)
    own = row_ids[:, None] == col_ids[None, :]
    left = jnp.where(own, statistic - statistic.astype(BF16).astype(F32), 0.0)
    low_here = lax.dynamic_update_slice(
        jnp.zeros((n,), F32), jnp.sum(left, axis=0), (col_start,)
    )
    low = lax.psum(low_here, ("row", "col"))
    wide = lax.all_gather(statistic.astype(BF16), "col", axis=1, tiled=True)
    whole = lax.all_gather(wide, "row", axis=0, tiled=True)
    prod = jnp.dot(whole, gradient, preferred_element_type=F32)
    pre = ((1.25 * gradient.astype(F32) - prod * (0.25 / scale4)) / root).astype(BF16)
    every = jnp.arange(n, dtype=jnp.int32)
    ident = row_ids[:, None] == every[None, :]
    r = (wide.astype(F32) + jnp.where(ident, low[None, :], 0.0)) / scale4
    for _ in range(4):
        prod = jnp.dot(r.astype(BF16), whole, preferred_element_type=F32)
        r = 1.25 * r - 0.25 * (prod + r * low[None, :]) / scale4
    next_diag = jnp.sum(jnp.where(ident, r, 0.0), axis=1)
    next_m = jnp.where(own, 0.0, lax.dynamic_slice_in_dim(r, col_start, cols_here, 1))
    return next_m, pre, next_diag


def solution(mesh):
    R, C = mesh.shape["row"], mesh.shape["col"]
    local = functools.partial(local_kernels, R, C) if C == 2 and R % C == 0 else local_plain
    return jax.shard_map(
        local,
        mesh=mesh,
        in_specs=(P(("section", "row"), "col"), P("section", ("row", "col"))),
        out_specs=(
            P(("section", "row"), "col"),
            P("section", ("row", "col")),
            P(("section", "row")),
        ),
        check_vma=False,
    )
```
